32 devices in a mesh: depth: 2 (over x), row: 4 (over y, core), col: 4 (over z).
Axes of the slice: x: 2, y: 2, z: 4, core: 2. Of those that a mesh axis runs over, the one named last changes fastest.
Arguments:
- x_out: float32 [8192, 768], P(('depth', 'col'), 'row'), may hold values from -6 to 6
- v_out: float32 [8192, 768], P(('depth', 'col'), 'row'), may hold values from -6 to 6
- dx_out: float32 [8192, 768], P(('depth', 'col'), 'row'), may hold values from -6 to 6
- dv_out: float32 [8192, 768], P(('depth', 'col'), 'row'), may hold values from -6 to 6
- gate_weight: bfloat16 [14336, 8192], P(('col', 'row'), 'depth'), may hold values from -0.0625 to 0.0625
- up_weight: bfloat16 [14336, 8192], P(('col', 'row'), 'depth'), may hold values from -0.0625 to 0.0625
- down_weight: bfloat16 [14336, 8192], P(('col', 'row'), 'depth'), may hold values from -0.046875 to 0.046875
Outputs:
- x_prev: float32 [8192, 768], P(('depth', 'col'), 'row')
- v_prev: float32 [8192, 768], P(('depth', 'col'), 'row')
- dx_prev: float32 [8192, 768], P(('depth', 'col'), 'row')
- grad_gate: float32 [14336, 8192], P(('col', 'row'), 'depth')
- grad_up: float32 [14336, 8192], P(('col', 'row'), 'depth')
- grad_down: float32 [14336, 8192], P(('col', 'row'), 'depth')
The draws below stay inside these ranges and needn't reach their ends.
All inputs are finite; a program needn't handle non-finite values.
Results may differ from the reference program's by a relative error of at most 0.0061.
Values may be sent and summed in bfloat16 or wider, within the bound.
A program may use at most 256 MiB of HBM per device.

```python
import jax
import jax.numpy as jnp

D = 8192
FF = 14336
TOKENS = 768


def block_scale(rng, dims, pieces, low, largest):
    def one(position, shards_of):
        steps = jax.random.uniform(jax.random.fold_in(jax.random.fold_in(rng, 6), position), (shards_of,), jnp.float32, low / len(pieces), largest / len(pieces))
        return jnp.repeat(jnp.exp(steps), dims[position] // shards_of).reshape((-1,) + (1,) * (len(dims) - position - 1))

    loudness = one(*pieces[0])
    for cut in pieces[1:]:
        loudness = loudness * one(*cut)
    return loudness


def bell_draw(key, dims, deviation, most, cuts=(), dtype=jnp.bfloat16):
    loudness = block_scale(key, dims, cuts, -0.22, 0.18) if cuts else 1.0
    entries = jax.random.normal(key, dims, jnp.float32) * deviation * loudness
    return jnp.minimum(jnp.maximum(entries, -most), most).astype(dtype)


def setup_inputs(seed: int = 0) -> dict:
    arg_keys = jax.random.split(jax.random.key(seed), 8)
    return {
        "x_out": bell_draw(arg_keys[0], (D, TOKENS), 1.0, 6.0, ((0, 8), (1, 4)), jnp.float32),
        "v_out": bell_draw(arg_keys[1], (D, TOKENS), 1.0, 6.0, ((0, 8), (1, 4)), jnp.float32),
        "dx_out": bell_draw(arg_keys[2], (D, TOKENS), 1.0, 6.0, ((0, 8), (1, 4)), jnp.float32),
        "dv_out": bell_draw(arg_keys[3], (D, TOKENS), 1.0, 6.0, ((0, 8), (1, 4)), jnp.float32),
        "gate_weight": bell_draw(arg_keys[4], (FF, D), D ** -0.5, 0.0625, ((0, 16), (1, 2))),
        "up_weight": bell_draw(arg_keys[5], (FF, D), D ** -0.5, 0.0625, ((0, 16), (1, 2))),
        "down_weight": bell_draw(arg_keys[6], (FF, D), FF ** -0.5, 0.046875, ((0, 16), (1, 2))),
    }


momentum = 0.5


def mult(left, right):
    return jnp.dot(left.astype(jnp.float32), right.astype(jnp.float32), preferred_element_type=jnp.float32)


def reference(x_out, v_out, dx_out, dv_out, gate_weight, up_weight, down_weight):
    x_prev = x_out - v_out
    x_half = x_prev.astype(jnp.bfloat16)
    df = ((1.0 - momentum) * (dx_out + dv_out)).astype(jnp.bfloat16)
    gate = mult(gate_weight, x_half)
    up = mult(up_weight, x_half)
    sig = jax.nn.sigmoid(gate)
    act = (gate * sig * up).astype(jnp.bfloat16)
    y_out = mult(down_weight.T, act)
    v_prev = (v_out - (1.0 - momentum) * y_out) / momentum
    d_act = mult(down_weight, df)
    d_gate = (d_act * up * sig * (1.0 + gate * (1.0 - sig))).astype(jnp.bfloat16)
    d_up = (d_act * gate * sig).astype(jnp.bfloat16)
    dx_prev = dx_out + (mult(gate_weight.T, d_gate) + mult(up_weight.T, d_up))
    grad_gate = mult(d_gate, x_half.T)
    grad_up = mult(d_up, x_half.T)
    grad_down = mult(act, df.T)
    return (x_prev, v_prev, dx_prev, grad_gate, grad_up, grad_down)
```

```python
import jax
import jax.numpy as jnp
from jax import lax
from jax.sharding import PartitionSpec as P

momentum = 0.5
CHUNKS = 3
BF = jnp.bfloat16
F32 = jnp.float32


def contract(left, right, left_dim, right_dim):
    return lax.dot_general(
        left, right, (((left_dim,), (right_dim,)), ((), ())), preferred_element_type=F32
    )


def swap(value, axis, mask):
    n = lax.axis_size(axis)
    return lax.ppermute(value, axis, [(i, i ^ mask) for i in range(n)])


def row_masks():
    masks, m = [], lax.axis_size("row") // 2
    while m:
        masks.append(m)
        m //= 2
    return masks


def gather_tokens(block):
    cols = lax.all_gather(block, "col", axis=0, tiled=False)
    n, t, f = cols.shape
    out = cols.transpose(1, 0, 2).reshape(t, n * f)
    for mask in row_masks():
        out = jnp.concatenate([out, swap(out, "row", mask)], axis=0)
    return out


def depth_sum(part):
    if lax.axis_size("depth") == 2:
        return part + swap(part.astype(BF), "depth", 1).astype(F32)
    return lax.psum(part, "depth")


def scatter_tokens(term):
    masks = row_masks()[::-1]
    total_rows = term.rows
    half = total_rows // 2
    got = swap(term(half, total_rows).astype(BF), "row", masks[0])
    kept = term(0, half) + got.astype(F32)
    for mask in masks[1:]:
        half //= 2
        got = swap(kept[half:].astype(BF), "row", mask)
        kept = kept[:half] + got.astype(F32)
    n = lax.axis_size("col")
    t, f = kept.shape
    blocks = kept.astype(BF).reshape(t, n, f // n).transpose(1, 0, 2)
    return lax.psum_scatter(blocks, "col", scatter_dimension=0, tiled=False)


class Term:
    def __init__(self, rows, fn):
        self.rows, self.fn = rows, fn

    def __call__(self, lo, hi):
        return self.fn(lo, hi)


def nonlinear(gate, up_val, d_act):
    sig = jax.nn.sigmoid(gate)
    act = (gate * sig * up_val).astype(BF)
    d_gate = (d_act * up_val * sig * (1.0 + gate * (1.0 - sig))).astype(BF)
    d_up = (d_act * gate * sig).astype(BF)
    return (act, d_gate, d_up)


def on_device(x_out, v_out, dx_out, dv_out, gate_weight, up_weight, down_weight):
    x_prev = x_out - v_out
    x_tok = x_prev.astype(BF).T
    df_tok = ((1.0 - momentum) * (dx_out + dv_out)).astype(BF).T
    tokens = x_tok.shape[0]
    t = tokens // CHUNKS
    xs, dfs, acts, dgates, dups, ys, dxs = [], [], [], [], [], [], []
    for c in range(CHUNKS):
        xs.append(gather_tokens(x_tok[c * t : (c + 1) * t]))
        dfs.append(gather_tokens(df_tok[c * t : (c + 1) * t]))
    for c in range(CHUNKS):
        gate = depth_sum(contract(xs[c], gate_weight, 1, 1))
        up_val = depth_sum(contract(xs[c], up_weight, 1, 1))
        d_act = depth_sum(contract(dfs[c], down_weight, 1, 1))
        act, d_gate, d_up = nonlinear(gate, up_val, d_act)
        acts.append(act)
        dgates.append(d_gate)
        dups.append(d_up)
        rows = act.shape[0]

        def down_term(lo, hi, act=act):
            return contract(act[lo:hi], down_weight, 1, 0)

        def input_term(lo, hi, d_gate=d_gate, d_up=d_up):
            return contract(d_gate[lo:hi], gate_weight, 1, 0) + contract(
                d_up[lo:hi], up_weight, 1, 0
            )

        ys.append(scatter_tokens(Term(rows, down_term)))
        dxs.append(scatter_tokens(Term(rows, input_term)))
    x_all, df_all = jnp.concatenate(xs, 0), jnp.concatenate(dfs, 0)
    grad_gate = contract(jnp.concatenate(dgates, 0), x_all, 0, 0)
    grad_up = contract(jnp.concatenate(dups, 0), x_all, 0, 0)
    grad_down = contract(jnp.concatenate(acts, 0), df_all, 0, 0)
    y_out = jnp.concatenate(ys, 0).astype(F32).T
    dx_sum = jnp.concatenate(dxs, 0).astype(F32).T
    v_prev = (v_out - (1.0 - momentum) * y_out) / momentum
    dx_prev = dx_out + dx_sum
    return (x_prev, v_prev, dx_prev, grad_gate, grad_up, grad_down)


def solution(mesh):
    act_spec, weight_spec = P(("depth", "col"), "row"), P(("col", "row"), "depth")
    return jax.shard_map(
        on_device,
        mesh=mesh,
        in_specs=(act_spec,) * 4 + (weight_spec,) * 3,
        out_specs=(act_spec,) * 3 + (weight_spec,) * 3,
        check_vma=False,
    )
```

```python
import jax
import jax.numpy as jnp
from jax import lax
from jax.sharding import PartitionSpec as P

momentum = 0.5
BF = jnp.bfloat16
F32 = jnp.float32


def contract(left, right, left_dim, right_dim):
    return lax.dot_general(
        left, right, (((left_dim,), (right_dim,)), ((), ())), preferred_element_type=F32
    )


def swap(value, axis, mask):
    n = lax.axis_size(axis)
    return lax.ppermute(value, axis, [(i, i ^ mask) for i in range(n)])


def merge_cols(cols):
    n, t, f = cols.shape
    return cols.transpose(1, 0, 2).reshape(t, n * f)


def gather_cols(block):
    return merge_cols(lax.all_gather(block, "col", axis=0, tiled=False))


def with_sibling(value):
    return jnp.concatenate([value, swap(value, "row", 1)], axis=0)


def depth_sum(part):
    return depth_sum_and_got(part)[0]


def depth_sum_and_got(part):
    if lax.axis_size("depth") == 2:
        got = swap(part.astype(BF), "depth", 1)
        return part + got.astype(F32), got
    total = lax.psum(part, "depth")
    return total, total


def fold_sibling(term, rows):
    got = swap(term(rows // 2, rows).astype(BF), "row", 1)
    return term(0, rows // 2) + got.astype(F32)


def scatter_sum(near, far):
    total = near + swap(far.astype(BF), "row", 2).astype(F32)
    n = lax.axis_size("col")
    t, f = total.shape
    blocks = total.astype(BF).reshape(t, n, f // n).transpose(1, 0, 2)
    return lax.psum_scatter(blocks, "col", scatter_dimension=0, tiled=False).astype(F32).T


def nonlinear(gate, up_val, d_act):
    sig = jax.nn.sigmoid(gate)
    act = (gate * sig * up_val).astype(BF)
    d_act, _ = lax.optimization_barrier((d_act, act))
    d_gate = (d_act * up_val * sig * (1.0 + gate * (1.0 - sig))).astype(BF)
    d_up = (d_act * gate * sig).astype(BF)
    return (act, d_gate, d_up)


def on_device(x_out, v_out, dx_out, dv_out, gate_weight, up_weight, down_weight):
    x_prev = x_out - v_out
    x_tok = x_prev.astype(BF).T
    df_tok = ((1.0 - momentum) * (dx_out + dv_out)).astype(BF).T
    x_near = gather_cols(x_tok)
    df_cols = lax.all_gather(df_tok, "col", axis=0, tiled=False)
    x_far = swap(x_near, "row", 2)
    x_pair = with_sibling(x_near)
    gate_near, gate_got = depth_sum_and_got(contract(x_pair, gate_weight, 1, 1))
    up_near = depth_sum(contract(x_pair, up_weight, 1, 1))
    df_cols, _ = lax.optimization_barrier((df_cols, gate_got))
    df_near = merge_cols(df_cols)
    xs = (x_pair, with_sibling(x_far))
    dfs = (with_sibling(df_near), with_sibling(swap(df_near, "row", 2)))
    gates = [gate_near, depth_sum(contract(xs[1], gate_weight, 1, 1))]
    ups = [up_near, depth_sum(contract(xs[1], up_weight, 1, 1))]
    d_acts = [depth_sum(contract(df, down_weight, 1, 1)) for df in dfs]
    rows = xs[0].shape[0]
    acts, dgates, dups = [], [], []
    ys, dxs = [], []
    for gate, up_val, d_act in zip(gates, ups, d_acts):
        act, d_gate, d_up = nonlinear(gate, up_val, d_act)
        acts.append(act)
        dgates.append(d_gate)
        dups.append(d_up)

        def down_term(lo, hi, act=act):
            return contract(act[lo:hi], down_weight, 1, 0)

        def input_term(lo, hi, d_gate=d_gate, d_up=d_up):
            return contract(d_gate[lo:hi], gate_weight, 1, 0) + contract(
                d_up[lo:hi], up_weight, 1, 0
            )

        ys.append(fold_sibling(down_term, rows))
        dxs.append(fold_sibling(input_term, rows))
    y_out = scatter_sum(*ys)
    dx_sum = scatter_sum(*dxs)
    x_all, df_all = jnp.concatenate(xs, 0), jnp.concatenate(dfs, 0)
    grad_gate = contract(jnp.concatenate(dgates, 0), x_all, 0, 0)
    grad_up = contract(jnp.concatenate(dups, 0), x_all, 0, 0)
    grad_down = contract(jnp.concatenate(acts, 0), df_all, 0, 0)
    v_prev = (v_out - (1.0 - momentum) * y_out) / momentum
    dx_prev = dx_out + dx_sum
    return (x_prev, v_prev, dx_prev, grad_gate, grad_up, grad_down)


def solution(mesh):
    act_spec, weight_spec = P(("depth", "col"), "row"), P(("col", "row"), "depth")
    return jax.shard_map(
        on_device,
        mesh=mesh,
        in_specs=(act_spec,) * 4 + (weight_spec,) * 3,
        out_specs=(act_spec,) * 3 + (weight_spec,) * 3,
        check_vma=False,
    )
```

```python
import jax
import jax.numpy as jnp
from jax import lax
from jax.sharding import PartitionSpec as P

momentum = 0.5
BF = jnp.bfloat16
F32 = jnp.float32


def contract(left, right, left_dim, right_dim):
    return lax.dot_general(
        left, right, (((left_dim,), (right_dim,)), ((), ())), preferred_element_type=F32
    )


def swap(value, axis, mask):
    n = lax.axis_size(axis)
    return lax.ppermute(value, axis, [(i, i ^ mask) for i in range(n)])


def merge_cols(cols):
    n, t, f = cols.shape
    return cols.transpose(1, 0, 2).reshape(t, n * f)


def gather_cols(block):
    return merge_cols(lax.all_gather(block, "col", axis=0, tiled=False))


def with_sibling(value):
    return jnp.concatenate([value, swap(value, "row", 1)], axis=0)


def depth_sum(part):
    return depth_sum_and_got(part)[0]


def depth_sum_and_got(part):
    if lax.axis_size("depth") == 2:
        got = swap(part.astype(BF), "depth", 1)
        return part + got.astype(F32), got
    total = lax.psum(part, "depth")
    return total, total


def fold_sibling(term, rows):
    got = swap(term(rows // 2, rows).astype(BF), "row", 1)
    return term(0, rows // 2) + got.astype(F32)


def scatter_sum(near, got):
    total = near + got.astype(F32)
    n = lax.axis_size("col")
    t, f = total.shape
    blocks = total.astype(BF).reshape(t, n, f // n).transpose(1, 0, 2)
    return lax.psum_scatter(blocks, "col", scatter_dimension=0, tiled=False).astype(F32).T


def after(value, earlier):
    return lax.optimization_barrier((value, earlier))[0]


def activation(gate, up_val):
    return (gate * jax.nn.sigmoid(gate) * up_val).astype(BF)


def cotangents(gate, up_val, d_act):
    sig = jax.nn.sigmoid(gate)
    d_gate = (d_act * up_val * sig * (1.0 + gate * (1.0 - sig))).astype(BF)
    d_up = (d_act * gate * sig).astype(BF)
    return (d_gate, d_up)


def on_device(x_out, v_out, dx_out, dv_out, gate_weight, up_weight, down_weight):
    x_prev = x_out - v_out
    x_tok = x_prev.astype(BF).T
    df_tok = ((1.0 - momentum) * (dx_out + dv_out)).astype(BF).T
    x_near = gather_cols(x_tok)
    df_cols = lax.all_gather(df_tok, "col", axis=0, tiled=False)
    x_far = swap(x_near, "row", 2)
    xa = with_sibling(x_near)
    gate_a, gate_got = depth_sum_and_got(contract(xa, gate_weight, 1, 1))
    up_a = depth_sum(contract(xa, up_weight, 1, 1))
    df_near = merge_cols(after(df_cols, gate_got))
    df_far = swap(df_near, "row", 2)
    xb, dfa, dfb = with_sibling(x_far), with_sibling(df_near), with_sibling(df_far)
    gate_b = depth_sum(contract(xb, gate_weight, 1, 1))
    up_b_part = contract(xb, up_weight, 1, 1)
    up_b = depth_sum(up_b_part)
    dact_a_part = contract(dfa, down_weight, 1, 1)
    dact_a = depth_sum(dact_a_part)
    dact_b_part = contract(dfb, down_weight, 1, 1)
    dact_b = depth_sum(dact_b_part)
    rows = xa.shape[0]

    def down_fold(act):
        return fold_sibling(lambda lo, hi: contract(act[lo:hi], down_weight, 1, 0), rows)

    def input_fold(d_gate, d_up):
        return fold_sibling(
            lambda lo, hi: contract(d_gate[lo:hi], gate_weight, 1, 0)
            + contract(d_up[lo:hi], up_weight, 1, 0),
            rows,
        )

    act_a = activation(gate_a, up_a)
    y_near = down_fold(after(after(act_a, up_b_part), dact_a_part))
    act_b = activation(gate_b, up_b)
    y_got = swap(down_fold(after(act_b, dact_b_part)).astype(BF), "row", 2)
    dgate_b, dup_b = cotangents(gate_b, up_b, after(dact_b, act_b))
    dx_far = input_fold(dgate_b, dup_b).astype(BF)
    dx_got = swap(dx_far, "row", 2)
    y_out = scatter_sum(y_near, after(y_got, dx_far))
    dgate_a, dup_a = cotangents(gate_a, up_a, after(dact_a, act_a))
    dx_near = input_fold(after(dgate_a, dx_far), dup_a)
    dx_sum = scatter_sum(dx_near, dx_got)
    xs, dfs = (xa, xb), (dfa, dfb)
    acts, dgates, dups = (act_a, act_b), (dgate_a, dgate_b), (dup_a, dup_b)
    x_all = after(jnp.concatenate(xs, 0), dx_far)
    df_all = after(jnp.concatenate(dfs, 0), dx_far)
    grad_gate = contract(jnp.concatenate(dgates, 0), x_all, 0, 0)
    grad_up = contract(jnp.concatenate(dups, 0), x_all, 0, 0)
    grad_down = contract(jnp.concatenate(acts, 0), df_all, 0, 0)
    v_prev = (v_out - (1.0 - momentum) * y_out) / momentum
    dx_prev = dx_out + dx_sum
    return (x_prev, v_prev, dx_prev, grad_gate, grad_up, grad_down)


def solution(mesh):
    act_spec, weight_spec = P(("depth", "col"), "row"), P(("col", "row"), "depth")
    return jax.shard_map(
        on_device,
        mesh=mesh,
        in_specs=(act_spec,) * 4 + (weight_spec,) * 3,
        out_specs=(act_spec,) * 3 + (weight_spec,) * 3,
        check_vma=False,
    )
```
